32 devices in a mesh: members: 2 (over x), wide: 8 (over z, y), narrow: 2 (over core).
Axes of the slice: x: 2, y: 2, z: 4, core: 2. Of those that a mesh axis runs over, the one named last changes fastest.
Arguments:
- coarse: bfloat16 [128, 128, 128], P(('members', 'wide')), parts along dimension 0, may hold values from -6 to 6
- wanted: int32 [8, 2, 8, 2], P('wide', 'narrow'), may hold values from -1 to 7, as said below
- intersection: int32 [512, 2, 4], P('wide', 'narrow'), may hold values from 0 to 15, as said below
- intersection_count: int32 [512, 2], P('wide', 'narrow'), may hold values from 1 to 4
- regrid_weight: bfloat16 [1024, 256, 4, 128], P('wide', 'narrow'), may hold values from -0.25 to 0.25
- reference_patch: bfloat16 [64, 512, 128], P(('wide', 'narrow')), may hold values from -300 to 300
- patch_index: int32 [256, 2], P('wide', 'narrow'), may hold values from 0 to 7
- query_weight: bfloat16 [128, 128], replicated, may hold values from -1 to 1
- key_value_weight: bfloat16 [128, 256], replicated, may hold values from -0.5 to 0.5
- out_weight: bfloat16 [128, 128], replicated, may hold values from -0.5 to 0.5
- conv_one: bfloat16 [3, 3, 128, 128], replicated, may hold values from -0.1875 to 0.1875
- conv_two: bfloat16 [3, 3, 128, 128], replicated, may hold values from -0.1875 to 0.1875
- gain_one: float32 [128], replicated, may hold values from 0.25 to 1.75
- gain_two: float32 [128], replicated, may hold values from 0.25 to 1.75
- gain_out: float32 [128], replicated, may hold values from 0.25 to 1.75
Outputs:
- fine_out: bfloat16 [2048, 256, 128], P(('members', 'wide'), 'narrow'), parts along dimension 0
The draws below stay inside these ranges and needn't reach their ends.
There are 2 independent parts, one for each index of `members`. The reference program is written for one: setup_inputs(seed, part) draws one part's arguments, and reference() takes and returns one part's arrays. A program takes and returns all parts, laid end to end along the dimension named above; an argument that names none is the same for every part. Nothing has to cross between parts.
Inputs may be any that keep to these rules, and one draw needn't show every extreme that they name: `wanted`: each entry is a block number held by holder o, or -1 for an empty slot; the live numbers of one (w, n, o) are distinct and come first; in every draw some (w, n, o) fill all 2 slots. `intersection`: every entry names a slot o * 2 + s whose wanted[w, n, o, s] is not -1, where w and n are the wide and narrow indices of the fine block.
All inputs are finite; a program needn't handle non-finite values.
Results may differ from the reference program's by a relative error of at most 0.012.
The reference program's roundings to bfloat16 on the way (of `regridded`, `queries`, `pair_table`, `weights`, `attended`, `carried`, `first_active` and `second_active`) count: a program that leaves them out, or rounds other values in their place, can miss the bound.
Values may be sent and summed in bfloat16 or wider, within the bound.
A program may use at most 256 MiB of HBM per device.

```python
import math
import jax
import jax.numpy as jnp
from jax import lax

C = 128
L = 4
CB = 128
CBD = 8
SLOT = 2
FR = 128
FC = 128
BR = 2
AR = 4
P_SIZE = 512
OWNERS = 8
COL_TILES = 2
NH = 1024
NW = 256
NCB = 64
NPATCH = 64
PGROUP = 8


def plan_counts(key):
    counts = jax.random.randint(jax.random.fold_in(key, 101), (OWNERS, COL_TILES, OWNERS), 1, SLOT + 1)
    holder_axis = jnp.arange(OWNERS, dtype=jnp.int32)
    forced = holder_axis[None, None, :] == (holder_axis[:, None, None] + 1) % OWNERS
    return jnp.where(forced, SLOT, counts).astype(jnp.int32)


def draw_wanted(key, part):
    counts = plan_counts(key)
    key = jax.random.fold_in(key, 7)
    scores = jax.random.randint(key, (OWNERS, COL_TILES, OWNERS, CBD), 0, 1 << 20) * CBD + jnp.arange(CBD, dtype=jnp.int32)
    picked = jnp.argsort(scores, axis=-1)[..., :SLOT].astype(jnp.int32)
    live = jnp.arange(SLOT, dtype=jnp.int32)[None, None, None, :] < counts[..., None]
    return jnp.where(live, picked, -1).astype(jnp.int32)


def draw_intersection(key, part):
    counts = plan_counts(key)
    key = jax.random.fold_in(key, 11)
    band_total = OWNERS * (FR // BR)
    holder_key, slot_key = jax.random.split(key)
    holder = jax.random.randint(holder_key, (band_total, COL_TILES, L), 0, OWNERS)
    requester = jnp.arange(band_total, dtype=jnp.int32) // (FR // BR)
    live_count = counts[requester[:, None, None], jnp.arange(COL_TILES, dtype=jnp.int32)[None, :, None], holder]
    within_slot = jax.random.randint(slot_key, (band_total, COL_TILES, L), 0, 1 << 20) % live_count
    return (holder * SLOT + within_slot).astype(jnp.int32)


def draw_reference_patch(key, part):
    key = jax.random.fold_in(key, 23)
    split_keys = jax.random.split(key, 1)
    return jnp.clip(jax.random.normal(split_keys[0], (NPATCH, P_SIZE, C), jnp.float32), -6.0, 6.0).astype(jnp.bfloat16)


def set_ends(values, own_key, least, high):
    index_at = [jax.random.randint(jax.random.fold_in(own_key, axis), (), 0, length) for axis, length in enumerate(values.shape)]
    longest = values.shape.index(max(values.shape))
    neighbour = index_at[:longest] + [(index_at[longest] + 1) % values.shape[longest]] + index_at[longest + 1:]
    return values.at[tuple(index_at)].set(least).at[tuple(neighbour)].set(high)


def steps_of(rng, shape, pieces, smallest, largest):
    factor_of, own = 1.0, jax.random.fold_in(rng, 6)
    for dim, blocks in pieces:
        heights = jnp.exp(jax.random.uniform(jax.random.fold_in(own, dim), (blocks,), jnp.float32, smallest / len(pieces), largest / len(pieces)))
        factor_of = factor_of * jnp.repeat(heights, shape[dim] // blocks).reshape([-1 if axis == dim else 1 for axis in range(len(shape))])
    return factor_of


def normal_values(stream_key, extent, scale, limit, shards=(), kind=jnp.bfloat16):
    values = scale * jax.random.normal(stream_key, extent, jnp.float32)
    if shards:
        values = values * steps_of(stream_key, extent, shards, -0.22, 0.18)
    return jnp.clip(values, -limit, limit).astype(kind)


def setup_inputs(seed: int = 0, part: int = 0) -> dict:
    splits = jax.random.split(jax.random.key(seed), 16)
    part_keys = jax.random.split(jax.random.fold_in(splits[15], part), 16)
    coarse = normal_values(part_keys[0], (NCB, CB, C), 1.0, 6.0, ((0, 8),))
    wanted = draw_wanted(jax.random.fold_in(splits[15], 71), part)
    intersection = draw_intersection(jax.random.fold_in(splits[15], 71), part)
    intersection_count = set_ends(jax.random.randint(splits[3], (NH // BR, COL_TILES), 1, L + 1), jax.random.fold_in(splits[3], 1), 1, L).astype(jnp.int32)
    regrid_weight = normal_values(splits[4], (NH, NW, L, CB), (L * CB) ** -0.5, 0.25, ((0, 8), (1, 2)))
    reference_patch = draw_reference_patch(jax.random.fold_in(splits[15], 71), part)
    patch_index = set_ends(jax.random.randint(splits[6], (NH // AR, COL_TILES), 0, PGROUP), jax.random.fold_in(splits[6], 1), 0, PGROUP - 1).astype(jnp.int32)
    query_weight = normal_values(splits[7], (C, C), (C // 4) ** -0.5, 1.0)
    key_value_weight = normal_values(splits[8], (C, 2 * C), C ** -0.5, 0.5)
    out_weight = normal_values(splits[9], (C, C), C ** -0.5, 0.5)
    conv_one = normal_values(splits[10], (3, 3, C, C), (9 * C) ** -0.5, 0.1875)
    conv_two = normal_values(splits[11], (3, 3, C, C), (9 * C) ** -0.5, 0.1875)
    gain_one = jnp.clip(1.0 + 0.15 * jax.random.normal(splits[12], (C,), jnp.float32), 0.25, 1.75)
    gain_two = jnp.clip(1.0 + 0.15 * jax.random.normal(splits[13], (C,), jnp.float32), 0.25, 1.75)
    gain_out = jnp.clip(1.0 + 0.15 * jax.random.normal(splits[14], (C,), jnp.float32), 0.25, 1.75)
    return dict(coarse=coarse, wanted=wanted, intersection=intersection, intersection_count=intersection_count, regrid_weight=regrid_weight, reference_patch=reference_patch, patch_index=patch_index, query_weight=query_weight, key_value_weight=key_value_weight, out_weight=out_weight, conv_one=conv_one, conv_two=conv_two, gain_one=gain_one, gain_two=gain_two, gain_out=gain_out)


def rms_scaled(values, scale_gain):
    mean_square = lax.optimization_barrier(jnp.mean(values * values, axis=-1, keepdims=True))
    return values * lax.rsqrt(mean_square + 1e-06) * scale_gain

def convolve_grid(active, kernel):
    padded = jnp.pad(active, ((1, 1), (1, 1), (0, 0)))
    height_cells, width_cells, channels = active.shape
    result = jnp.zeros((height_cells * width_cells, kernel.shape[3]), jnp.float32)
    for offset_row in range(3):
        for offset_col in range(3):
            window = padded[offset_row:offset_row + height_cells, offset_col:offset_col + width_cells, :]
            result = result + jnp.dot(window.reshape(height_cells * width_cells, channels), kernel[offset_row, offset_col], preferred_element_type=jnp.float32)
    return result

def reference(coarse, wanted, intersection, intersection_count, regrid_weight, reference_patch, patch_index, query_weight, key_value_weight, out_weight, conv_one, conv_two, gain_one, gain_two, gain_out):
    band_total = NH // BR
    holder = intersection // SLOT
    within_slot = intersection % SLOT
    requester = (jnp.arange(band_total, dtype=jnp.int32) // (FR // BR))[:, None, None]
    column_tile = jnp.arange(COL_TILES, dtype=jnp.int32)[None, :, None]
    block_id = (holder * CBD + wanted[requester, column_tile, holder, within_slot]).astype(jnp.int32)
    entry_live = jnp.arange(L, dtype=jnp.int32)[None, None, :] < intersection_count[:, :, None]
    band_weight = regrid_weight.reshape(band_total, BR, COL_TILES, FC, L * CB).transpose(0, 2, 1, 3, 4).reshape(band_total, COL_TILES, BR * FC, L * CB)

    def regrid_band(inputs):
        weight_piece, id_piece, live_piece = inputs
        blocks = coarse[id_piece]
        blocks = jnp.where(live_piece[:, :, None, None], blocks, jnp.zeros((), blocks.dtype))
        stacked = blocks.reshape(COL_TILES, L * CB, C).astype(jnp.float32)
        return jnp.einsum('npk,nkc->npc', weight_piece.astype(jnp.float32), stacked, precision=lax.Precision.HIGHEST)
    regrid_bands = lax.map(regrid_band, (band_weight, block_id, entry_live))
    regridded = regrid_bands.reshape(band_total, COL_TILES, BR, FC, C).transpose(0, 2, 1, 3, 4).reshape(NH * NW, C).astype(jnp.bfloat16)
    regridded = lax.optimization_barrier(regridded)
    queries = jnp.dot(regridded, query_weight, preferred_element_type=jnp.float32).astype(jnp.bfloat16)
    queries = lax.optimization_barrier(queries)
    pair_table = jnp.dot(reference_patch.reshape(NPATCH * P_SIZE, C), key_value_weight, preferred_element_type=jnp.float32).astype(jnp.bfloat16)
    pair_table = lax.optimization_barrier(pair_table).reshape(NPATCH, P_SIZE, 2 * C)
    tile_total = NH // AR
    query_tiles = queries.reshape(tile_total, AR, COL_TILES, FC, C).transpose(0, 2, 1, 3, 4).reshape(tile_total, COL_TILES, AR * FC, C)
    group_start = jnp.arange(tile_total, dtype=jnp.int32) // (FR // AR) * PGROUP
    patch_global = (group_start[:, None] + patch_index).astype(jnp.int32)
    score_scale = 1.0 / math.sqrt(C)

    def attend_band(inputs):
        band_queries, band_patches = inputs
        chosen = pair_table[band_patches]
        key_part = chosen[:, :, :C].astype(jnp.float32)
        value_part = chosen[:, :, C:].astype(jnp.float32)
        scores = jnp.einsum('nqc,nkc->nqk', band_queries.astype(jnp.float32), key_part, precision=lax.Precision.HIGHEST) * score_scale
        row_peak = lax.optimization_barrier(jnp.max(scores, axis=-1, keepdims=True))
        lifted = jnp.exp(scores - row_peak)
        denominator = lax.optimization_barrier(jnp.sum(lifted, axis=-1, keepdims=True))
        weights = lax.optimization_barrier(lifted.astype(jnp.bfloat16))
        attended = jnp.einsum('nqk,nkc->nqc', weights.astype(jnp.float32), value_part, precision=lax.Precision.HIGHEST) / denominator
        return attended.astype(jnp.bfloat16)
    attended_tiles = lax.map(attend_band, (query_tiles, patch_global))
    attended = attended_tiles.reshape(tile_total, COL_TILES, AR, FC, C).transpose(0, 2, 1, 3, 4).reshape(NH * NW, C)
    mixed = jnp.dot(attended, out_weight, preferred_element_type=jnp.float32)
    carried = (regridded.astype(jnp.float32) + mixed).astype(jnp.bfloat16)
    carried = lax.optimization_barrier(carried).astype(jnp.float32)
    first_active = jax.nn.silu(rms_scaled(carried, gain_one)).astype(jnp.bfloat16)
    first_conv = convolve_grid(first_active.reshape(NH, NW, C), conv_one)
    second_active = jax.nn.silu(rms_scaled(first_conv, gain_two)).astype(jnp.bfloat16)
    second_conv = convolve_grid(second_active.reshape(NH, NW, C), conv_two)
    fine_out = rms_scaled(carried + second_conv, gain_out).astype(jnp.bfloat16)
    return fine_out.reshape(NH, NW, C)
```

```python
import functools
import math

import jax
import jax.numpy as jnp
from jax import lax
from jax.experimental import pallas as pl
from jax.experimental.pallas import tpu as pltpu
from jax.sharding import PartitionSpec as P

BR = 2
AR = 4
SIDE = 16
LOG2E = 1.4426950408889634


def rms_scaled(values, scale_gain):
    mean_square = jnp.mean(values * values, axis=-1, keepdims=True)
    return values * lax.rsqrt(mean_square + 1e-06) * scale_gain


def silu(values):
    half = values * 0.5
    return half + half * jnp.tanh(half)


def attend_kernel(
    wanted,
    lists,
    counts,
    patches,
    weight,
    blocks,
    patch,
    query_weight,
    key_value_weight,
    out_weight,
    gain,
    carried,
    active,
    keys,
    values,
    *,
    per_step,
    entries,
    slots,
    held,
    fine_cols,
):
    step = pl.program_id(0)
    channels = blocks.shape[2]

    @pl.when(step == 0)
    def _():
        def one(index, carry):
            cells = patch[index]
            keys[index] = lax.dot_general(
                key_value_weight[:, :channels],
                cells,
                (((0,), (1,)), ((), ())),
                preferred_element_type=jnp.float32,
            ).astype(jnp.bfloat16)
            values[index, :, :channels] = jnp.dot(
                cells, key_value_weight[:, channels:], preferred_element_type=jnp.float32
            ).astype(jnp.bfloat16)
            values[index, :, channels:] = jnp.ones(cells.shape, jnp.bfloat16)
            return carry

        lax.fori_loop(0, patch.shape[0], one, 0)

    band_cells = BR * fine_cols
    tile_cells = AR * fine_cols
    bands = AR // BR
    factor = LOG2E / math.sqrt(channels)
    for local in range(per_step):
        tile = step * per_step + local
        pieces = []
        for band in range(bands):
            row = tile * bands + band
            used = counts[row]
            first = local * tile_cells + band * band_cells
            stacked = []
            for entry in range(entries):
                listed = lists[row * entries + entry]
                block = (listed // slots) * held + jnp.maximum(wanted[listed], 0)
                cells = blocks[block]
                stacked.append(jnp.where(entry < used, cells, jnp.zeros_like(cells)))
            spread = jnp.concatenate(
                [weight[first : first + band_cells, entry, :] for entry in range(entries)], axis=1
            )
            pieces.append(
                jnp.dot(
                    spread, jnp.concatenate(stacked, axis=0), preferred_element_type=jnp.float32
                ).astype(jnp.bfloat16)
            )
        regridded = jnp.concatenate(pieces, axis=0)
        queries = jnp.dot(
            regridded, query_weight[...], preferred_element_type=jnp.float32
        ).astype(jnp.bfloat16)
        chosen = patches[tile]
        scores = jnp.dot(queries, keys[chosen], preferred_element_type=jnp.float32)
        peak = jnp.max(scores, axis=-1, keepdims=True)
        lifted = jnp.exp2((scores - peak) * factor).astype(jnp.bfloat16)
        summed = jnp.dot(lifted, values[chosen], preferred_element_type=jnp.float32)
        attended = (summed[:, :channels] / summed[:, channels:]).astype(jnp.bfloat16)
        mixed = jnp.dot(attended, out_weight[...], preferred_element_type=jnp.float32)
        total = (regridded.astype(jnp.float32) + mixed).astype(jnp.bfloat16)
        where_to = pl.ds(local * tile_cells, tile_cells)
        carried[where_to, :] = total
        active[where_to, :] = silu(
            rms_scaled(total.astype(jnp.float32), gain[...])
        ).astype(jnp.bfloat16)


def attend(
    wanted, lists, counts, patches, weight, blocks, patch, query_weight, key_value_weight,
    out_weight, gain, held, slots, fine_cols,
):
    cells, entries, _ = weight.shape
    channels = blocks.shape[2]
    tile_cells = AR * fine_cols
    per_step = 2
    step_cells = per_step * tile_cells
    smem = pl.BlockSpec(memory_space=pltpu.SMEM)
    vmem = pl.BlockSpec(memory_space=pltpu.VMEM)
    out = jax.ShapeDtypeStruct((cells, channels), jnp.bfloat16)
    out_spec = pl.BlockSpec((step_cells, channels), lambda s: (s, 0))
    return pl.pallas_call(
        functools.partial(
            attend_kernel,
            per_step=per_step,
            entries=entries,
            slots=slots,
            held=held,
            fine_cols=fine_cols,
        ),
        grid=(cells // step_cells,),
        out_shape=(out, out),
        in_specs=[smem] * 4
        + [pl.BlockSpec((step_cells, entries, weight.shape[2]), lambda s: (s, 0, 0))]
        + [vmem] * 6,
        out_specs=(out_spec, out_spec),
        scratch_shapes=[
            pltpu.VMEM((patch.shape[0], channels, patch.shape[1]), jnp.bfloat16),
            pltpu.VMEM((patch.shape[0], patch.shape[1], 2 * channels), jnp.bfloat16),
        ],
        compiler_params=pltpu.CompilerParams(vmem_limit_bytes=48 * 1024 * 1024),
        name="attend",
    )(
        wanted, lists, counts, patches, weight, blocks, patch, query_weight, key_value_weight,
        out_weight, gain,
    )


def spread_taps(taps, wide_taps):
    channels = taps.shape[2]
    wide_taps[...] = jnp.zeros(wide_taps.shape, wide_taps.dtype)
    for column in range(3):
        for row in range(3):
            for out_row in range(2):
                wide_taps[
                    column,
                    (row + out_row) * channels : (row + out_row + 1) * channels,
                    out_row * channels : (out_row + 1) * channels,
                ] = taps[row, column]


def convolve(source, first, rows, wide_taps):
    width, channels = source.shape[1:]
    pairs = rows // 2
    slabs = [source[first + index] for index in range(rows + 2)]
    stacked = jnp.concatenate(
        [
            jnp.concatenate([slabs[2 * pair + shift] for shift in range(4)], axis=1)
            for pair in range(pairs)
        ],
        axis=0,
    )
    total = None
    for column, turn in ((1, 0), (0, 1), (2, width - 1)):
        part = jnp.dot(stacked, wide_taps[column], preferred_element_type=jnp.float32)
        part = part.reshape(pairs, width, 2 * channels)
        if turn:
            part = pltpu.roll(part, turn, 1)
        total = part if total is None else total + part
    return total


def conv_kernel(
    active, above, below, side, carried, taps_one, taps_two, gain_two, gain_out, out,
    padded, second, wide_one, wide_two, *, rows_one, rows_two,
):
    fine_rows, fine_cols, channels = active.shape
    width = padded.shape[1]
    spread_taps(taps_one, wide_one)
    spread_taps(taps_two, wide_two)
    padded[0:2, :fine_cols, :] = above[...]
    padded[fine_rows + 2 : fine_rows + 4, :fine_cols, :] = below[...]
    padded[:, fine_cols:, :] = side[...]

    def fill(index, carry):
        first = index * 8
        padded[pl.ds(first + 2, 8), :fine_cols, :] = active[pl.ds(first, 8)]
        return carry

    lax.fori_loop(0, fine_rows // 8, fill, 0)
    band = lax.axis_index("wide")
    part = lax.axis_index("narrow")
    column = lax.broadcasted_iota(jnp.int32, (1, width, channels), 1)
    left = (part > 0).astype(jnp.int32)
    right = (part < lax.axis_size("narrow") - 1).astype(jnp.int32)
    keep = (column < fine_cols + right) | (column >= width - left)

    def first_conv(index, carry):
        first = index * rows_one
        total = convolve(padded, first, rows_one, wide_one)
        for half in range(2):
            piece = total[:, :, half * channels : (half + 1) * channels]
            piece = silu(rms_scaled(piece, gain_two[...]))
            piece = jnp.where(keep, piece, 0.0).astype(jnp.bfloat16)
            for pair in range(rows_one // 2):
                second[first + 2 * pair + half] = piece[pair]
        return carry

    lax.fori_loop(0, (fine_rows + 2) // rows_one, first_conv, 0)

    @pl.when(band == 0)
    def _():
        second[0] = jnp.zeros((width, channels), jnp.bfloat16)

    @pl.when(band == lax.axis_size("wide") - 1)
    def _():
        second[fine_rows + 1] = jnp.zeros((width, channels), jnp.bfloat16)

    def second_conv(index, carry):
        first = index * rows_two
        total = convolve(second, first, rows_two, wide_two)
        for half in range(2):
            for pair in range(rows_two // 2):
                row = first + 2 * pair + half
                piece = total[pair, :fine_cols, half * channels : (half + 1) * channels]
                piece = piece + carried[row].astype(jnp.float32)
                out[row] = rms_scaled(piece, gain_out[...]).astype(jnp.bfloat16)
        return carry

    lax.fori_loop(0, fine_rows // rows_two, second_conv, 0)


def convolutions(active, above, below, side, carried, taps_one, taps_two, gain_two, gain_out):
    fine_rows, fine_cols, channels = active.shape
    width = fine_cols + SIDE
    vmem = pl.BlockSpec(memory_space=pltpu.VMEM)
    return pl.pallas_call(
        functools.partial(conv_kernel, rows_one=10, rows_two=8),
        out_shape=jax.ShapeDtypeStruct(active.shape, jnp.bfloat16),
        in_specs=[vmem] * 9,
        out_specs=vmem,
        scratch_shapes=[
            pltpu.VMEM((fine_rows + 4, width, channels), jnp.bfloat16),
            pltpu.VMEM((fine_rows + 2, width, channels), jnp.bfloat16),
            pltpu.VMEM((3, 4 * channels, 2 * channels), jnp.bfloat16),
            pltpu.VMEM((3, 4 * channels, 2 * channels), jnp.bfloat16),
        ],
        compiler_params=pltpu.CompilerParams(vmem_limit_bytes=56 * 1024 * 1024),
        name="convolutions",
    )(active, above, below, side, carried, taps_one, taps_two, gain_two, gain_out)


def from_both(cells, axis, dim, width):
    count = lax.axis_size(axis)
    ends = count - 1
    head = lax.slice_in_dim(cells, 0, width, axis=dim)
    tail = lax.slice_in_dim(cells, cells.shape[dim] - width, cells.shape[dim], axis=dim)
    before = lax.ppermute(tail, axis, [(i, i + 1) for i in range(ends)])
    after = lax.ppermute(head, axis, [(i + 1, i) for i in range(ends)])
    return before, after


def on_device(
    coarse,
    wanted,
    intersection,
    intersection_count,
    regrid_weight,
    reference_patch,
    patch_index,
    query_weight,
    key_value_weight,
    out_weight,
    conv_one,
    conv_two,
    gain_one,
    gain_two,
    gain_out,
):
    slot_count = wanted.shape[3]
    channels = coarse.shape[2]
    fine_rows, fine_cols, entries, block_cells = regrid_weight.shape
    every_block = lax.all_gather(coarse, "wide", axis=0, tiled=True)
    group_patch = lax.all_gather(reference_patch, "narrow", axis=0, tiled=True)
    carried, active = attend(
        wanted.reshape(-1),
        intersection.reshape(-1),
        intersection_count.reshape(-1),
        patch_index.reshape(-1),
        regrid_weight.reshape(fine_rows * fine_cols, entries, block_cells),
        every_block,
        group_patch,
        query_weight,
        key_value_weight,
        out_weight,
        gain_one.reshape(1, channels),
        coarse.shape[0],
        slot_count,
        fine_cols,
    )
    carried = carried.reshape(fine_rows, fine_cols, channels)
    active = active.reshape(fine_rows, fine_cols, channels)
    above, below = from_both(active, "wide", 0, 2)
    edges = jnp.concatenate(
        [
            jnp.concatenate([rows[:, :2], rows[:, fine_cols - 2 :]], axis=1)
            for rows in (above, active, below)
        ],
        axis=0,
    )
    before, after = from_both(edges, "narrow", 1, 2)
    middle = jnp.zeros((fine_rows + 4, SIDE - 4, channels), jnp.bfloat16)
    side = jnp.concatenate([after, middle, before], axis=1)
    return convolutions(
        active,
        above,
        below,
        side,
        carried,
        conv_one,
        conv_two,
        gain_two.reshape(1, channels),
        gain_out.reshape(1, channels),
    )


def solution(mesh):
    placed = (
        P(("members", "wide"), None, None),
        P("wide", "narrow", None, None),
        P("wide", "narrow", None),
        P("wide", "narrow"),
        P("wide", "narrow", None, None),
        P(("wide", "narrow"), None, None),
        P("wide", "narrow"),
        P(),
        P(),
        P(),
        P(),
        P(),
        P(),
        P(),
        P(),
    )
    return jax.shard_map(
        on_device,
        mesh=mesh,
        in_specs=placed,
        out_specs=P(("members", "wide"), "narrow", None),
        check_vma=False,
    )
```

```python
import functools
import math

import jax
import jax.numpy as jnp
from jax import lax
from jax.experimental import pallas as pl
from jax.experimental.pallas import tpu as pltpu
from jax.sharding import PartitionSpec as P

BR = 2
AR = 4
SIDE = 16
LOG2E = 1.4426950408889634


def rms_scaled(values, scale_gain):
    mean_square = jnp.mean(values * values, axis=-1, keepdims=True)
    return values * lax.rsqrt(mean_square + 1e-06) * scale_gain


def silu(values):
    half = values * 0.5
    return half + half * jnp.tanh(half)


def gather_kernel(
    coarse, patch, blocks, patches, send_right, send_left, recv_right, recv_left,
    pass_send, pass_recv, patch_sem, own_sem,
):
    ring = lax.axis_size("wide")
    held = coarse.shape[0]
    share = held // 2
    group = patch.shape[0]
    here = lax.axis_index("wide")
    core = lax.axis_index("narrow")
    level = here // 2
    place = level + (here % 2) * (ring - 1 - 2 * level)

    def index_of(spot):
        upper = spot // (ring // 2)
        return 2 * spot + upper * (2 * ring - 1 - 4 * spot)

    right = {"wide": index_of((place + 1) % ring)}
    left = {"wide": index_of((place + ring - 1) % ring)}
    other = {"narrow": 1 - core}
    barrier = pltpu.get_barrier_semaphore()
    for target in (right, left, other):
        pl.semaphore_signal(
            barrier, inc=1, device_id=target, device_id_type=pl.DeviceIdType.MESH
        )
    pl.semaphore_wait(barrier, 3)

    def rows(spot):
        return pl.ds(index_of(spot) * held + core * share, share)

    def send(source, target, send_sem, recv_sem, device):
        return pltpu.make_async_remote_copy(
            src_ref=source,
            dst_ref=target,
            send_sem=send_sem,
            recv_sem=recv_sem,
            device_id=device,
            device_id_type=pl.DeviceIdType.MESH,
        )

    right_steps, left_steps = ring // 2, (ring - 1) // 2
    own = coarse.at[pl.ds(core * share, share)]
    mine = blocks.at[rows(place)]
    going_right = [send(own, mine, send_right.at[0], recv_right.at[0], right)]
    going_left = [send(own, mine, send_left.at[0], recv_left.at[0], left)]
    going_right[0].start()
    going_left[0].start()
    across = send(
        patch,
        patches.at[pl.ds(core * group, group)],
        patch_sem.at[0],
        patch_sem.at[1],
        other,
    )
    across.start()
    own_blocks = pltpu.make_async_copy(coarse, blocks.at[pl.ds(here * held, held)], own_sem.at[0])
    own_blocks.start()
    own_patch = pltpu.make_async_copy(
        patch, patches.at[pl.ds(core * group, group)], own_sem.at[1]
    )
    own_patch.start()
    passed = []
    for step in range(right_steps):
        going_right[step].wait_recv()
        landed = blocks.at[rows((place + ring - 1 - step) % ring)]
        if step + 1 < right_steps:
            copy = send(
                landed, landed, send_right.at[step + 1], recv_right.at[step + 1], right
            )
            copy.start()
            going_right.append(copy)
        copy = send(landed, landed, pass_send.at[len(passed)], pass_recv.at[len(passed)], other)
        copy.start()
        passed.append(copy)
        if step < left_steps:
            going_left[step].wait_recv()
            landed = blocks.at[rows((place + 1 + step) % ring)]
            if step + 1 < left_steps:
                copy = send(
                    landed, landed, send_left.at[step + 1], recv_left.at[step + 1], left
                )
                copy.start()
                going_left.append(copy)
            copy = send(
                landed, landed, pass_send.at[len(passed)], pass_recv.at[len(passed)], other
            )
            copy.start()
            passed.append(copy)
    for copy in going_right + going_left:
        copy.wait_send()
    for copy in passed:
        copy.wait()
    across.wait()
    own_blocks.wait()
    own_patch.wait()


def gather(coarse, patch):
    ring = lax.axis_size("wide")
    right_steps, left_steps = ring // 2, (ring - 1) // 2
    dma = pltpu.SemaphoreType.DMA
    anywhere = pl.BlockSpec(memory_space=pl.ANY)
    return pl.pallas_call(
        gather_kernel,
        out_shape=(
            jax.ShapeDtypeStruct((ring * coarse.shape[0],) + coarse.shape[1:], coarse.dtype),
            jax.ShapeDtypeStruct((2 * patch.shape[0],) + patch.shape[1:], patch.dtype),
        ),
        in_specs=[anywhere] * 2,
        out_specs=(anywhere, anywhere),
        scratch_shapes=[
            dma((right_steps,)),
            dma((left_steps,)),
            dma((right_steps,)),
            dma((left_steps,)),
            dma((ring - 1,)),
            dma((ring - 1,)),
            dma((2,)),
            dma((2,)),
        ],
        compiler_params=pltpu.CompilerParams(collective_id=0, has_side_effects=True),
        name="gather",
    )(coarse, patch)


def attend_kernel(
    wanted,
    lists,
    counts,
    patches,
    weight,
    blocks,
    patch,
    query_weight,
    key_value_weight,
    out_weight,
    gain,
    carried,
    active,
    keys,
    values,
    *,
    per_step,
    entries,
    slots,
    held,
    fine_cols,
):
    step = pl.program_id(0)
    channels = blocks.shape[2]

    @pl.when(step == 0)
    def _():
        def one(index, carry):
            cells = patch[index]
            keys[index] = lax.dot_general(
                key_value_weight[:, :channels],
                cells,
                (((0,), (1,)), ((), ())),
                preferred_element_type=jnp.float32,
            ).astype(jnp.bfloat16)
            values[index, :, :channels] = jnp.dot(
                cells, key_value_weight[:, channels:], preferred_element_type=jnp.float32
            ).astype(jnp.bfloat16)
            values[index, :, channels:] = jnp.ones(cells.shape, jnp.bfloat16)
            return carry

        lax.fori_loop(0, patch.shape[0], one, 0)

    band_cells = BR * fine_cols
    tile_cells = AR * fine_cols
    bands = AR // BR
    factor = LOG2E / math.sqrt(channels)
    for local in range(per_step):
        tile = step * per_step + local
        pieces = []
        for band in range(bands):
            row = tile * bands + band
            used = counts[row]
            first = local * tile_cells + band * band_cells
            stacked = []
            for entry in range(entries):
                listed = lists[row * entries + entry]
                block = (listed // slots) * held + jnp.maximum(wanted[listed], 0)
                cells = blocks[block]
                stacked.append(jnp.where(entry < used, cells, jnp.zeros_like(cells)))
            spread = jnp.concatenate(
                [weight[first : first + band_cells, entry, :] for entry in range(entries)], axis=1
            )
            pieces.append(
                jnp.dot(
                    spread, jnp.concatenate(stacked, axis=0), preferred_element_type=jnp.float32
                ).astype(jnp.bfloat16)
            )
        regridded = jnp.concatenate(pieces, axis=0)
        queries = jnp.dot(
            regridded, query_weight[...], preferred_element_type=jnp.float32
        ).astype(jnp.bfloat16)
        chosen = patches[tile]
        scores = jnp.dot(queries, keys[chosen], preferred_element_type=jnp.float32)
        peak = jnp.max(scores, axis=-1, keepdims=True)
        lifted = jnp.exp2((scores - peak) * factor).astype(jnp.bfloat16)
        summed = jnp.dot(lifted, values[chosen], preferred_element_type=jnp.float32)
        attended = (summed[:, :channels] / summed[:, channels:]).astype(jnp.bfloat16)
        mixed = jnp.dot(attended, out_weight[...], preferred_element_type=jnp.float32)
        total = (regridded.astype(jnp.float32) + mixed).astype(jnp.bfloat16)
        where_to = pl.ds(local * tile_cells, tile_cells)
        carried[where_to, :] = total
        active[where_to, :] = silu(
            rms_scaled(total.astype(jnp.float32), gain[...])
        ).astype(jnp.bfloat16)


def attend(
    wanted, lists, counts, patches, weight, blocks, patch, query_weight, key_value_weight,
    out_weight, gain, held, slots, fine_cols,
):
    cells, entries, _ = weight.shape
    channels = blocks.shape[2]
    tile_cells = AR * fine_cols
    per_step = 2
    step_cells = per_step * tile_cells
    smem = pl.BlockSpec(memory_space=pltpu.SMEM)
    vmem = pl.BlockSpec(memory_space=pltpu.VMEM)
    out = jax.ShapeDtypeStruct((cells, channels), jnp.bfloat16)
    out_spec = pl.BlockSpec((step_cells, channels), lambda s: (s, 0))
    return pl.pallas_call(
        functools.partial(
            attend_kernel,
            per_step=per_step,
            entries=entries,
            slots=slots,
            held=held,
            fine_cols=fine_cols,
        ),
        grid=(cells // step_cells,),
        out_shape=(out, out),
        in_specs=[smem] * 4
        + [pl.BlockSpec((step_cells, entries, weight.shape[2]), lambda s: (s, 0, 0))]
        + [vmem] * 6,
        out_specs=(out_spec, out_spec),
        scratch_shapes=[
            pltpu.VMEM((patch.shape[0], channels, patch.shape[1]), jnp.bfloat16),
            pltpu.VMEM((patch.shape[0], patch.shape[1], 2 * channels), jnp.bfloat16),
        ],
        compiler_params=pltpu.CompilerParams(vmem_limit_bytes=48 * 1024 * 1024),
        name="attend",
    )(
        wanted, lists, counts, patches, weight, blocks, patch, query_weight, key_value_weight,
        out_weight, gain,
    )


def spread_taps(taps, wide_taps):
    channels = taps.shape[2]
    wide_taps[...] = jnp.zeros(wide_taps.shape, wide_taps.dtype)
    for column in range(3):
        for row in range(3):
            for out_row in range(2):
                wide_taps[
                    column,
                    (row + out_row) * channels : (row + out_row + 1) * channels,
                    out_row * channels : (out_row + 1) * channels,
                ] = taps[row, column]


def convolve(source, first, rows, wide_taps):
    width, channels = source.shape[1:]
    pairs = rows // 2
    slabs = [source[first + index] for index in range(rows + 2)]
    stacked = jnp.concatenate(
        [
            jnp.concatenate([slabs[2 * pair + shift] for shift in range(4)], axis=1)
            for pair in range(pairs)
        ],
        axis=0,
    )
    total = None
    for column, turn in ((1, 0), (0, 1), (2, width - 1)):
        part = jnp.dot(stacked, wide_taps[column], preferred_element_type=jnp.float32)
        part = part.reshape(pairs, width, 2 * channels)
        if turn:
            part = pltpu.roll(part, turn, 1)
        total = part if total is None else total + part
    return total


def conv_kernel(
    active, above, below, side, carried, taps_one, taps_two, gain_two, gain_out, out,
    padded, second, wide_one, wide_two, *, rows_one, rows_two,
):
    fine_rows, fine_cols, channels = active.shape
    width = padded.shape[1]
    spread_taps(taps_one, wide_one)
    spread_taps(taps_two, wide_two)
    padded[0:2, :fine_cols, :] = above[...]
    padded[fine_rows + 2 : fine_rows + 4, :fine_cols, :] = below[...]
    padded[:, fine_cols:, :] = side[...]

    def fill(index, carry):
        first = index * 8
        padded[pl.ds(first + 2, 8), :fine_cols, :] = active[pl.ds(first, 8)]
        return carry

    lax.fori_loop(0, fine_rows // 8, fill, 0)
    band = lax.axis_index("wide")
    part = lax.axis_index("narrow")
    column = lax.broadcasted_iota(jnp.int32, (1, width, channels), 1)
    left = (part > 0).astype(jnp.int32)
    right = (part < lax.axis_size("narrow") - 1).astype(jnp.int32)
    keep = (column < fine_cols + right) | (column >= width - left)

    def first_conv(index, carry):
        first = index * rows_one
        total = convolve(padded, first, rows_one, wide_one)
        for half in range(2):
            piece = total[:, :, half * channels : (half + 1) * channels]
            piece = silu(rms_scaled(piece, gain_two[...]))
            piece = jnp.where(keep, piece, 0.0).astype(jnp.bfloat16)
            for pair in range(rows_one // 2):
                second[first + 2 * pair + half] = piece[pair]
        return carry

    lax.fori_loop(0, (fine_rows + 2) // rows_one, first_conv, 0)

    @pl.when(band == 0)
    def _():
        second[0] = jnp.zeros((width, channels), jnp.bfloat16)

    @pl.when(band == lax.axis_size("wide") - 1)
    def _():
        second[fine_rows + 1] = jnp.zeros((width, channels), jnp.bfloat16)

    def second_conv(index, carry):
        first = index * rows_two
        total = convolve(second, first, rows_two, wide_two)
        for half in range(2):
            for pair in range(rows_two // 2):
                row = first + 2 * pair + half
                piece = total[pair, :fine_cols, half * channels : (half + 1) * channels]
                piece = piece + carried[row].astype(jnp.float32)
                out[row] = rms_scaled(piece, gain_out[...]).astype(jnp.bfloat16)
        return carry

    lax.fori_loop(0, fine_rows // rows_two, second_conv, 0)


def convolutions(active, above, below, side, carried, taps_one, taps_two, gain_two, gain_out):
    fine_rows, fine_cols, channels = active.shape
    width = fine_cols + SIDE
    vmem = pl.BlockSpec(memory_space=pltpu.VMEM)
    return pl.pallas_call(
        functools.partial(conv_kernel, rows_one=10, rows_two=8),
        out_shape=jax.ShapeDtypeStruct(active.shape, jnp.bfloat16),
        in_specs=[vmem] * 9,
        out_specs=vmem,
        scratch_shapes=[
            pltpu.VMEM((fine_rows + 4, width, channels), jnp.bfloat16),
            pltpu.VMEM((fine_rows + 2, width, channels), jnp.bfloat16),
            pltpu.VMEM((3, 4 * channels, 2 * channels), jnp.bfloat16),
            pltpu.VMEM((3, 4 * channels, 2 * channels), jnp.bfloat16),
        ],
        compiler_params=pltpu.CompilerParams(vmem_limit_bytes=56 * 1024 * 1024),
        name="convolutions",
    )(active, above, below, side, carried, taps_one, taps_two, gain_two, gain_out)


def from_both(cells, axis, dim, width):
    count = lax.axis_size(axis)
    ends = count - 1
    head = lax.slice_in_dim(cells, 0, width, axis=dim)
    tail = lax.slice_in_dim(cells, cells.shape[dim] - width, cells.shape[dim], axis=dim)
    before = lax.ppermute(tail, axis, [(i, i + 1) for i in range(ends)])
    after = lax.ppermute(head, axis, [(i + 1, i) for i in range(ends)])
    return before, after


def on_device(
    coarse,
    wanted,
    intersection,
    intersection_count,
    regrid_weight,
    reference_patch,
    patch_index,
    query_weight,
    key_value_weight,
    out_weight,
    conv_one,
    conv_two,
    gain_one,
    gain_two,
    gain_out,
):
    slot_count = wanted.shape[3]
    channels = coarse.shape[2]
    fine_rows, fine_cols, entries, block_cells = regrid_weight.shape
    every_block, group_patch = gather(coarse, reference_patch)
    carried, active = attend(
        wanted.reshape(-1),
        intersection.reshape(-1),
        intersection_count.reshape(-1),
        patch_index.reshape(-1),
        regrid_weight.reshape(fine_rows * fine_cols, entries, block_cells),
        every_block,
        group_patch,
        query_weight,
        key_value_weight,
        out_weight,
        gain_one.reshape(1, channels),
        coarse.shape[0],
        slot_count,
        fine_cols,
    )
    carried = carried.reshape(fine_rows, fine_cols, channels)
    active = active.reshape(fine_rows, fine_cols, channels)
    above, below = from_both(active, "wide", 0, 2)
    edges = jnp.concatenate(
        [
            jnp.concatenate([rows[:, :2], rows[:, fine_cols - 2 :]], axis=1)
            for rows in (above, active, below)
        ],
        axis=0,
    )
    before, after = from_both(edges, "narrow", 1, 2)
    middle = jnp.zeros((fine_rows + 4, SIDE - 4, channels), jnp.bfloat16)
    side = jnp.concatenate([after, middle, before], axis=1)
    return convolutions(
        active,
        above,
        below,
        side,
        carried,
        conv_one,
        conv_two,
        gain_two.reshape(1, channels),
        gain_out.reshape(1, channels),
    )


def solution(mesh):
    placed = (
        P(("members", "wide"), None, None),
        P("wide", "narrow", None, None),
        P("wide", "narrow", None),
        P("wide", "narrow"),
        P("wide", "narrow", None, None),
        P(("wide", "narrow"), None, None),
        P("wide", "narrow"),
        P(),
        P(),
        P(),
        P(),
        P(),
        P(),
        P(),
        P(),
    )
    return jax.shard_map(
        on_device,
        mesh=mesh,
        in_specs=placed,
        out_specs=P(("members", "wide"), "narrow", None),
        check_vma=False,
    )
```

```python
import functools
import math

import jax
import jax.numpy as jnp
from jax import lax
from jax.experimental import pallas as pl
from jax.experimental.pallas import tpu as pltpu
from jax.sharding import PartitionSpec as P

BR = 2
AR = 4
SIDE = 16
LOG2E = 1.4426950408889634


def rms_scaled(values, scale_gain):
    mean_square = jnp.mean(values * values, axis=-1, keepdims=True)
    return values * lax.rsqrt(mean_square + 1e-06) * scale_gain


def silu(values):
    half = values * 0.5
    return half + half * jnp.tanh(half)


def gather_kernel(
    coarse, patch, blocks, patches, send_right, send_left, recv_right, recv_left,
    pass_send, pass_recv, patch_sem, own_sem,
):
    ring = lax.axis_size("wide")
    held = coarse.shape[0]
    share = held // 2
    group = patch.shape[0]
    here = lax.axis_index("wide")
    core = lax.axis_index("narrow")
    level = here // 2
    place = level + (here % 2) * (ring - 1 - 2 * level)

    def index_of(spot):
        upper = spot // (ring // 2)
        return 2 * spot + upper * (2 * ring - 1 - 4 * spot)

    right = {"wide": index_of((place + 1) % ring)}
    left = {"wide": index_of((place + ring - 1) % ring)}
    other = {"narrow": 1 - core}
    barrier = pltpu.get_barrier_semaphore()
    for target in (right, left, other):
        pl.semaphore_signal(
            barrier, inc=1, device_id=target, device_id_type=pl.DeviceIdType.MESH
        )
    pl.semaphore_wait(barrier, 3)

    def rows(spot):
        return pl.ds(index_of(spot) * held + core * share, share)

    def send(source, target, send_sem, recv_sem, device):
        return pltpu.make_async_remote_copy(
            src_ref=source,
            dst_ref=target,
            send_sem=send_sem,
            recv_sem=recv_sem,
            device_id=device,
            device_id_type=pl.DeviceIdType.MESH,
        )

    right_steps, left_steps = ring // 2, (ring - 1) // 2
    own = coarse.at[pl.ds(core * share, share)]
    mine = blocks.at[rows(place)]
    going_right = [send(own, mine, send_right.at[0], recv_right.at[0], right)]
    going_left = [send(own, mine, send_left.at[0], recv_left.at[0], left)]
    going_right[0].start()
    going_left[0].start()
    across = send(
        patch,
        patches.at[pl.ds(core * group, group)],
        patch_sem.at[0],
        patch_sem.at[1],
        other,
    )
    across.start()
    own_blocks = pltpu.make_async_copy(coarse, blocks.at[pl.ds(here * held, held)], own_sem.at[0])
    own_blocks.start()
    own_patch = pltpu.make_async_copy(
        patch, patches.at[pl.ds(core * group, group)], own_sem.at[1]
    )
    own_patch.start()
    passed = []
    for step in range(right_steps):
        going_right[step].wait_recv()
        landed = blocks.at[rows((place + ring - 1 - step) % ring)]
        if step + 1 < right_steps:
            copy = send(
                landed, landed, send_right.at[step + 1], recv_right.at[step + 1], right
            )
            copy.start()
            going_right.append(copy)
        copy = send(landed, landed, pass_send.at[len(passed)], pass_recv.at[len(passed)], other)
        copy.start()
        passed.append(copy)
        if step < left_steps:
            going_left[step].wait_recv()
            landed = blocks.at[rows((place + 1 + step) % ring)]
            if step + 1 < left_steps:
                copy = send(
                    landed, landed, send_left.at[step + 1], recv_left.at[step + 1], left
                )
                copy.start()
                going_left.append(copy)
            copy = send(
                landed, landed, pass_send.at[len(passed)], pass_recv.at[len(passed)], other
            )
            copy.start()
            passed.append(copy)
    for copy in going_right + going_left:
        copy.wait_send()
    for copy in passed:
        copy.wait()
    across.wait()
    own_blocks.wait()
    own_patch.wait()


def gather(coarse, patch):
    ring = lax.axis_size("wide")
    right_steps, left_steps = ring // 2, (ring - 1) // 2
    dma = pltpu.SemaphoreType.DMA
    anywhere = pl.BlockSpec(memory_space=pl.ANY)
    return pl.pallas_call(
        gather_kernel,
        out_shape=(
            jax.ShapeDtypeStruct((ring * coarse.shape[0],) + coarse.shape[1:], coarse.dtype),
            jax.ShapeDtypeStruct((2 * patch.shape[0],) + patch.shape[1:], patch.dtype),
        ),
        in_specs=[anywhere] * 2,
        out_specs=(anywhere, anywhere),
        scratch_shapes=[
            dma((right_steps,)),
            dma((left_steps,)),
            dma((right_steps,)),
            dma((left_steps,)),
            dma((ring - 1,)),
            dma((ring - 1,)),
            dma((2,)),
            dma((2,)),
        ],
        compiler_params=pltpu.CompilerParams(collective_id=0, has_side_effects=True),
        name="gather",
    )(coarse, patch)


def attend_kernel(
    wanted,
    lists,
    counts,
    patches,
    weight,
    blocks,
    patch,
    query_weight,
    key_value_weight,
    out_weight,
    gain,
    carried,
    active,
    keys,
    values,
    *,
    per_step,
    entries,
    slots,
    held,
    fine_cols,
):
    step = pl.program_id(0)
    channels = blocks.shape[2]

    @pl.when(step == 0)
    def _():
        def one(index, carry):
            cells = patch[index]
            keys[index] = lax.dot_general(
                key_value_weight[:, :channels],
                cells,
                (((0,), (1,)), ((), ())),
                preferred_element_type=jnp.float32,
            ).astype(jnp.bfloat16)
            values[index, :, :channels] = jnp.dot(
                cells, key_value_weight[:, channels:], preferred_element_type=jnp.float32
            ).astype(jnp.bfloat16)
            values[index, :, channels:] = jnp.ones(cells.shape, jnp.bfloat16)
            return carry

        lax.fori_loop(0, patch.shape[0], one, 0)

    band_cells = BR * fine_cols
    tile_cells = AR * fine_cols
    bands = AR // BR
    factor = LOG2E / math.sqrt(channels)
    for local in range(per_step):
        tile = step * per_step + local
        pieces = []
        for band in range(bands):
            row = tile * bands + band
            used = counts[row]
            first = local * tile_cells + band * band_cells
            stacked = []
            for entry in range(entries):
                listed = lists[row * entries + entry]
                block = (listed // slots) * held + jnp.maximum(wanted[listed], 0)
                cells = blocks[block]
                stacked.append(jnp.where(entry < used, cells, jnp.zeros_like(cells)))
            spread = (
                weight[first : first + band_cells]
                .astype(jnp.float32)
                .reshape(band_cells, entries * weight.shape[2])
                .astype(jnp.bfloat16)
            )
            pieces.append(
                jnp.dot(
                    spread, jnp.concatenate(stacked, axis=0), preferred_element_type=jnp.float32
                ).astype(jnp.bfloat16)
            )
        regridded = jnp.concatenate(pieces, axis=0)
        queries = jnp.dot(
            regridded, query_weight[...], preferred_element_type=jnp.float32
        ).astype(jnp.bfloat16)
        chosen = patches[tile]
        scores = jnp.dot(queries, keys[chosen], preferred_element_type=jnp.float32)
        peak = jnp.max(scores, axis=-1, keepdims=True)
        lifted = jnp.exp2((scores - peak) * factor).astype(jnp.bfloat16)
        summed = jnp.dot(lifted, values[chosen], preferred_element_type=jnp.float32)
        attended = (summed[:, :channels] / summed[:, channels:]).astype(jnp.bfloat16)
        mixed = jnp.dot(attended, out_weight[...], preferred_element_type=jnp.float32)
        total = (regridded.astype(jnp.float32) + mixed).astype(jnp.bfloat16)
        where_to = pl.ds(local * tile_cells, tile_cells)
        carried[where_to, :] = total
        active[where_to, :] = silu(
            rms_scaled(total.astype(jnp.float32), gain[...])
        ).astype(jnp.bfloat16)


def attend(
    wanted, lists, counts, patches, weight, blocks, patch, query_weight, key_value_weight,
    out_weight, gain, held, slots, fine_cols,
):
    cells, entries, _ = weight.shape
    channels = blocks.shape[2]
    tile_cells = AR * fine_cols
    per_step = 2
    step_cells = per_step * tile_cells
    smem = pl.BlockSpec(memory_space=pltpu.SMEM)
    vmem = pl.BlockSpec(memory_space=pltpu.VMEM)
    out = jax.ShapeDtypeStruct((cells, channels), jnp.bfloat16)
    out_spec = pl.BlockSpec((step_cells, channels), lambda s: (s, 0))
    return pl.pallas_call(
        functools.partial(
            attend_kernel,
            per_step=per_step,
            entries=entries,
            slots=slots,
            held=held,
            fine_cols=fine_cols,
        ),
        grid=(cells // step_cells,),
        out_shape=(out, out),
        in_specs=[smem] * 4
        + [pl.BlockSpec((step_cells, entries, weight.shape[2]), lambda s: (s, 0, 0))]
        + [vmem] * 6,
        out_specs=(out_spec, out_spec),
        scratch_shapes=[
            pltpu.VMEM((patch.shape[0], channels, patch.shape[1]), jnp.bfloat16),
            pltpu.VMEM((patch.shape[0], patch.shape[1], 2 * channels), jnp.bfloat16),
        ],
        compiler_params=pltpu.CompilerParams(vmem_limit_bytes=48 * 1024 * 1024),
        name="attend",
    )(
        wanted, lists, counts, patches, weight, blocks, patch, query_weight, key_value_weight,
        out_weight, gain,
    )


def spread_taps(taps, wide_taps):
    channels = taps.shape[2]
    wide_taps[...] = jnp.zeros(wide_taps.shape, wide_taps.dtype)
    for column in range(3):
        for row in range(3):
            for out_row in range(2):
                wide_taps[
                    column,
                    (row + out_row) * channels : (row + out_row + 1) * channels,
                    out_row * channels : (out_row + 1) * channels,
                ] = taps[row, column]


def convolve(source, first, rows, wide_taps):
    width, channels = source.shape[1:]
    pairs = rows // 2
    slabs = [source[first + index] for index in range(rows + 2)]
    stacked = jnp.concatenate(
        [
            jnp.concatenate([slabs[2 * pair + shift] for shift in range(4)], axis=1)
            for pair in range(pairs)
        ],
        axis=0,
    )
    total = None
    for column, turn in ((1, 0), (0, 1), (2, width - 1)):
        part = jnp.dot(stacked, wide_taps[column], preferred_element_type=jnp.float32)
        part = part.reshape(pairs, width, 2 * channels)
        if turn:
            part = pltpu.roll(part, turn, 1)
        total = part if total is None else total + part
    return total


def conv_kernel(
    active, above, below, side, carried, taps_one, taps_two, gain_two, gain_out, out,
    padded, second, wide_one, wide_two, *, rows_one, rows_two,
):
    fine_rows, fine_cols, channels = active.shape
    width = padded.shape[1]
    spread_taps(taps_one, wide_one)
    spread_taps(taps_two, wide_two)
    padded[0:2, :fine_cols, :] = above[...]
    padded[fine_rows + 2 : fine_rows + 4, :fine_cols, :] = below[...]
    padded[:, fine_cols:, :] = side[...]

    def fill(index, carry):
        first = index * 8
        padded[pl.ds(first + 2, 8), :fine_cols, :] = active[pl.ds(first, 8)]
        return carry

    lax.fori_loop(0, fine_rows // 8, fill, 0)
    band = lax.axis_index("wide")
    part = lax.axis_index("narrow")
    column = lax.broadcasted_iota(jnp.int32, (1, width, channels), 1)
    left = (part > 0).astype(jnp.int32)
    right = (part < lax.axis_size("narrow") - 1).astype(jnp.int32)
    keep = (column < fine_cols + right) | (column >= width - left)

    def first_conv(index, carry):
        first = index * rows_one
        total = convolve(padded, first, rows_one, wide_one)
        for half in range(2):
            piece = total[:, :, half * channels : (half + 1) * channels]
            piece = silu(rms_scaled(piece, gain_two[...]))
            piece = jnp.where(keep, piece, 0.0).astype(jnp.bfloat16)
            for pair in range(rows_one // 2):
                second[first + 2 * pair + half] = piece[pair]
        return carry

    lax.fori_loop(0, (fine_rows + 2) // rows_one, first_conv, 0)

    @pl.when(band == 0)
    def _():
        second[0] = jnp.zeros((width, channels), jnp.bfloat16)

    @pl.when(band == lax.axis_size("wide") - 1)
    def _():
        second[fine_rows + 1] = jnp.zeros((width, channels), jnp.bfloat16)

    def second_conv(index, carry):
        first = index * rows_two
        total = convolve(second, first, rows_two, wide_two)
        for half in range(2):
            for pair in range(rows_two // 2):
                row = first + 2 * pair + half
                piece = total[pair, :fine_cols, half * channels : (half + 1) * channels]
                piece = piece + carried[row].astype(jnp.float32)
                out[row] = rms_scaled(piece, gain_out[...]).astype(jnp.bfloat16)
        return carry

    lax.fori_loop(0, fine_rows // rows_two, second_conv, 0)


def convolutions(active, above, below, side, carried, taps_one, taps_two, gain_two, gain_out):
    fine_rows, fine_cols, channels = active.shape
    width = fine_cols + SIDE
    vmem = pl.BlockSpec(memory_space=pltpu.VMEM)
    return pl.pallas_call(
        functools.partial(conv_kernel, rows_one=10, rows_two=8),
        out_shape=jax.ShapeDtypeStruct(active.shape, jnp.bfloat16),
        in_specs=[vmem] * 9,
        out_specs=vmem,
        scratch_shapes=[
            pltpu.VMEM((fine_rows + 4, width, channels), jnp.bfloat16),
            pltpu.VMEM((fine_rows + 2, width, channels), jnp.bfloat16),
            pltpu.VMEM((3, 4 * channels, 2 * channels), jnp.bfloat16),
            pltpu.VMEM((3, 4 * channels, 2 * channels), jnp.bfloat16),
        ],
        compiler_params=pltpu.CompilerParams(vmem_limit_bytes=56 * 1024 * 1024),
        name="convolutions",
    )(active, above, below, side, carried, taps_one, taps_two, gain_two, gain_out)


def from_both(cells, axis, dim, width):
    count = lax.axis_size(axis)
    ends = count - 1
    head = lax.slice_in_dim(cells, 0, width, axis=dim)
    tail = lax.slice_in_dim(cells, cells.shape[dim] - width, cells.shape[dim], axis=dim)
    before = lax.ppermute(tail, axis, [(i, i + 1) for i in range(ends)])
    after = lax.ppermute(head, axis, [(i + 1, i) for i in range(ends)])
    return before, after


def on_device(
    coarse,
    wanted,
    intersection,
    intersection_count,
    regrid_weight,
    reference_patch,
    patch_index,
    query_weight,
    key_value_weight,
    out_weight,
    conv_one,
    conv_two,
    gain_one,
    gain_two,
    gain_out,
):
    slot_count = wanted.shape[3]
    channels = coarse.shape[2]
    fine_rows, fine_cols, entries, block_cells = regrid_weight.shape
    every_block, group_patch = gather(coarse, reference_patch)
    carried, active = attend(
        wanted.reshape(-1),
        intersection.reshape(-1),
        intersection_count.reshape(-1),
        patch_index.reshape(-1),
        regrid_weight.reshape(fine_rows * fine_cols, entries, block_cells),
        every_block,
        group_patch,
        query_weight,
        key_value_weight,
        out_weight,
        gain_one.reshape(1, channels),
        coarse.shape[0],
        slot_count,
        fine_cols,
    )
    carried = carried.reshape(fine_rows, fine_cols, channels)
    active = active.reshape(fine_rows, fine_cols, channels)
    above, below = from_both(active, "wide", 0, 2)
    edges = jnp.concatenate(
        [
            jnp.concatenate([rows[:, :2], rows[:, fine_cols - 2 :]], axis=1)
            for rows in (above, active, below)
        ],
        axis=0,
    )
    before, after = from_both(edges, "narrow", 1, 2)
    middle = jnp.zeros((fine_rows + 4, SIDE - 4, channels), jnp.bfloat16)
    side = jnp.concatenate([after, middle, before], axis=1)
    return convolutions(
        active,
        above,
        below,
        side,
        carried,
        conv_one,
        conv_two,
        gain_two.reshape(1, channels),
        gain_out.reshape(1, channels),
    )


def solution(mesh):
    placed = (
        P(("members", "wide"), None, None),
        P("wide", "narrow", None, None),
        P("wide", "narrow", None),
        P("wide", "narrow"),
        P("wide", "narrow", None, None),
        P(("wide", "narrow"), None, None),
        P("wide", "narrow"),
        P(),
        P(),
        P(),
        P(),
        P(),
        P(),
        P(),
        P(),
    )
    return jax.shard_map(
        on_device,
        mesh=mesh,
        in_specs=placed,
        out_specs=P(("members", "wide"), "narrow", None),
        check_vma=False,
    )
```

```python
import functools
import math

import jax
import jax.numpy as jnp
from jax import lax
from jax.experimental import pallas as pl
from jax.experimental.pallas import tpu as pltpu
from jax.sharding import PartitionSpec as P

BR = 2
AR = 4
SIDE = 16
LOG2E = 1.4426950408889634


def rms_scaled(values, scale_gain):
    mean_square = jnp.mean(values * values, axis=-1, keepdims=True)
    return values * lax.rsqrt(mean_square + 1e-06) * scale_gain


def silu(values):
    half = values * 0.5
    return half + half * jnp.tanh(half)


def gather_kernel(
    coarse, patch, blocks, patches, send_right, send_left, recv_right, recv_left,
    pass_send, pass_recv, patch_sem, own_sem,
):
    ring = lax.axis_size("wide")
    held = coarse.shape[0]
    share = held // 2
    group = patch.shape[0]
    here = lax.axis_index("wide")
    core = lax.axis_index("narrow")
    level = here // 2
    place = level + (here % 2) * (ring - 1 - 2 * level)

    def index_of(spot):
        upper = spot // (ring // 2)
        return 2 * spot + upper * (2 * ring - 1 - 4 * spot)

    right = {"wide": index_of((place + 1) % ring)}
    left = {"wide": index_of((place + ring - 1) % ring)}
    other = {"narrow": 1 - core}
    barrier = pltpu.get_barrier_semaphore()
    for target in (right, left, other):
        pl.semaphore_signal(
            barrier, inc=1, device_id=target, device_id_type=pl.DeviceIdType.MESH
        )
    pl.semaphore_wait(barrier, 3)

    def rows(spot):
        return pl.ds(index_of(spot) * held + core * share, share)

    def send(source, target, send_sem, recv_sem, device):
        return pltpu.make_async_remote_copy(
            src_ref=source,
            dst_ref=target,
            send_sem=send_sem,
            recv_sem=recv_sem,
            device_id=device,
            device_id_type=pl.DeviceIdType.MESH,
        )

    right_steps, left_steps = ring // 2, (ring - 1) // 2
    own = coarse.at[pl.ds(core * share, share)]
    mine = blocks.at[rows(place)]
    going_right = [send(own, mine, send_right.at[0], recv_right.at[0], right)]
    going_left = [send(own, mine, send_left.at[0], recv_left.at[0], left)]
    going_right[0].start()
    going_left[0].start()
    across = send(
        patch,
        patches.at[pl.ds(core * group, group)],
        patch_sem.at[0],
        patch_sem.at[1],
        other,
    )
    across.start()
    own_blocks = pltpu.make_async_copy(coarse, blocks.at[pl.ds(here * held, held)], own_sem.at[0])
    own_blocks.start()
    own_patch = pltpu.make_async_copy(
        patch, patches.at[pl.ds(core * group, group)], own_sem.at[1]
    )
    own_patch.start()
    passed = []
    for step in range(right_steps):
        going_right[step].wait_recv()
        landed = blocks.at[rows((place + ring - 1 - step) % ring)]
        if step + 1 < right_steps:
            copy = send(
                landed, landed, send_right.at[step + 1], recv_right.at[step + 1], right
            )
            copy.start()
            going_right.append(copy)
        copy = send(landed, landed, pass_send.at[len(passed)], pass_recv.at[len(passed)], other)
        copy.start()
        passed.append(copy)
        if step < left_steps:
            going_left[step].wait_recv()
            landed = blocks.at[rows((place + 1 + step) % ring)]
            if step + 1 < left_steps:
                copy = send(
                    landed, landed, send_left.at[step + 1], recv_left.at[step + 1], left
                )
                copy.start()
                going_left.append(copy)
            copy = send(
                landed, landed, pass_send.at[len(passed)], pass_recv.at[len(passed)], other
            )
            copy.start()
            passed.append(copy)
    for copy in going_right + going_left:
        copy.wait_send()
    for copy in passed:
        copy.wait()
    across.wait()
    own_blocks.wait()
    own_patch.wait()


def gather(coarse, patch):
    ring = lax.axis_size("wide")
    right_steps, left_steps = ring // 2, (ring - 1) // 2
    dma = pltpu.SemaphoreType.DMA
    anywhere = pl.BlockSpec(memory_space=pl.ANY)
    return pl.pallas_call(
        gather_kernel,
        out_shape=(
            jax.ShapeDtypeStruct((ring * coarse.shape[0],) + coarse.shape[1:], coarse.dtype),
            jax.ShapeDtypeStruct((2 * patch.shape[0],) + patch.shape[1:], patch.dtype),
        ),
        in_specs=[anywhere] * 2,
        out_specs=(anywhere, anywhere),
        scratch_shapes=[
            dma((right_steps,)),
            dma((left_steps,)),
            dma((right_steps,)),
            dma((left_steps,)),
            dma((ring - 1,)),
            dma((ring - 1,)),
            dma((2,)),
            dma((2,)),
        ],
        compiler_params=pltpu.CompilerParams(collective_id=0, has_side_effects=True),
        name="gather",
    )(coarse, patch)


def attend_kernel(
    wanted,
    lists,
    counts,
    patches,
    weight,
    blocks,
    patch,
    query_weight,
    key_value_weight,
    out_weight,
    gain,
    carried,
    active,
    keys,
    values,
    *,
    per_step,
    entries,
    slots,
    held,
    fine_cols,
):
    step = pl.program_id(0)
    channels = blocks.shape[2]

    @pl.when(step == 0)
    def _():
        def one(index, carry):
            cells = patch[index]
            keys[index] = lax.dot_general(
                key_value_weight[:, :channels],
                cells,
                (((0,), (1,)), ((), ())),
                preferred_element_type=jnp.float32,
            ).astype(jnp.bfloat16)
            values[index, :, :channels] = jnp.dot(
                cells, key_value_weight[:, channels:], preferred_element_type=jnp.float32
            ).astype(jnp.bfloat16)
            values[index, :, channels:] = jnp.ones(cells.shape, jnp.bfloat16)
            return carry

        lax.fori_loop(0, patch.shape[0], one, 0)

    band_cells = BR * fine_cols
    tile_cells = AR * fine_cols
    bands = AR // BR
    factor = LOG2E / math.sqrt(channels)
    for local in range(per_step):
        tile = step * per_step + local
        pieces = []
        for band in range(bands):
            row = tile * bands + band
            used = counts[row]
            first = local * tile_cells + band * band_cells
            stacked = []
            for entry in range(entries):
                listed = lists[row * entries + entry]
                block = (listed // slots) * held + jnp.maximum(wanted[listed], 0)
                cells = blocks[block]
                stacked.append(jnp.where(entry < used, cells, jnp.zeros_like(cells)))
            spread = (
                weight[first : first + band_cells]
                .astype(jnp.float32)
                .reshape(band_cells, entries * weight.shape[2])
                .astype(jnp.bfloat16)
            )
            pieces.append(
                jnp.dot(
                    spread, jnp.concatenate(stacked, axis=0), preferred_element_type=jnp.float32
                ).astype(jnp.bfloat16)
            )
        regridded = jnp.concatenate(pieces, axis=0)
        queries = jnp.dot(
            regridded, query_weight[...], preferred_element_type=jnp.float32
        ).astype(jnp.bfloat16)
        chosen = patches[tile]
        scores = jnp.dot(queries, keys[chosen], preferred_element_type=jnp.float32)
        peak = jnp.max(scores, axis=-1, keepdims=True)
        lifted = jnp.exp2((scores - peak) * factor).astype(jnp.bfloat16)
        summed = jnp.dot(lifted, values[chosen], preferred_element_type=jnp.float32)
        attended = (summed[:, :channels] / summed[:, channels:]).astype(jnp.bfloat16)
        mixed = jnp.dot(attended, out_weight[...], preferred_element_type=jnp.float32)
        total = (regridded.astype(jnp.float32) + mixed).astype(jnp.bfloat16)
        where_to = pl.ds(local * tile_cells, tile_cells)
        carried[where_to, :] = total
        active[where_to, :] = silu(
            rms_scaled(total.astype(jnp.float32), gain[...])
        ).astype(jnp.bfloat16)


def attend(
    wanted, lists, counts, patches, weight, blocks, patch, query_weight, key_value_weight,
    out_weight, gain, held, slots, fine_cols,
):
    cells, entries, _ = weight.shape
    channels = blocks.shape[2]
    tile_cells = AR * fine_cols
    per_step = 4
    step_cells = per_step * tile_cells
    smem = pl.BlockSpec(memory_space=pltpu.SMEM)
    vmem = pl.BlockSpec(memory_space=pltpu.VMEM)
    out = jax.ShapeDtypeStruct((cells, channels), jnp.bfloat16)
    out_spec = pl.BlockSpec((step_cells, channels), lambda s: (s, 0))
    return pl.pallas_call(
        functools.partial(
            attend_kernel,
            per_step=per_step,
            entries=entries,
            slots=slots,
            held=held,
            fine_cols=fine_cols,
        ),
        grid=(cells // step_cells,),
        out_shape=(out, out),
        in_specs=[smem] * 4
        + [pl.BlockSpec((step_cells, entries, weight.shape[2]), lambda s: (s, 0, 0))]
        + [vmem] * 6,
        out_specs=(out_spec, out_spec),
        scratch_shapes=[
            pltpu.VMEM((patch.shape[0], channels, patch.shape[1]), jnp.bfloat16),
            pltpu.VMEM((patch.shape[0], patch.shape[1], 2 * channels), jnp.bfloat16),
        ],
        compiler_params=pltpu.CompilerParams(vmem_limit_bytes=48 * 1024 * 1024),
        name="attend",
    )(
        wanted, lists, counts, patches, weight, blocks, patch, query_weight, key_value_weight,
        out_weight, gain,
    )


def spread_taps(taps, wide_taps):
    channels = taps.shape[2]
    wide_taps[...] = jnp.zeros(wide_taps.shape, wide_taps.dtype)
    for column in range(3):
        for row in range(3):
            for out_row in range(2):
                wide_taps[
                    column,
                    (row + out_row) * channels : (row + out_row + 1) * channels,
                    out_row * channels : (out_row + 1) * channels,
                ] = taps[row, column]


def convolve(source, first, rows, wide_taps):
    width, channels = source.shape[1:]
    pairs = rows // 2
    slabs = [source[first + index] for index in range(rows + 2)]
    stacked = jnp.concatenate(
        [
            jnp.concatenate([slabs[2 * pair + shift] for shift in range(4)], axis=1)
            for pair in range(pairs)
        ],
        axis=0,
    )
    total = None
    for column, turn in ((1, 0), (0, 1), (2, width - 1)):
        part = jnp.dot(stacked, wide_taps[column], preferred_element_type=jnp.float32)
        part = part.reshape(pairs, width, 2 * channels)
        if turn:
            part = pltpu.roll(part, turn, 1)
        total = part if total is None else total + part
    return total


def conv_kernel(
    active, above, below, side, carried, taps_one, taps_two, gain_two, gain_out, out,
    padded, second, wide_one, wide_two, *, rows_one, rows_two,
):
    fine_rows, fine_cols, channels = active.shape
    width = padded.shape[1]
    spread_taps(taps_one, wide_one)
    spread_taps(taps_two, wide_two)
    padded[0:2, :fine_cols, :] = above[...]
    padded[fine_rows + 2 : fine_rows + 4, :fine_cols, :] = below[...]
    padded[:, fine_cols:, :] = side[...]

    def fill(index, carry):
        first = index * 8
        padded[pl.ds(first + 2, 8), :fine_cols, :] = active[pl.ds(first, 8)]
        return carry

    lax.fori_loop(0, fine_rows // 8, fill, 0)
    band = lax.axis_index("wide")
    part = lax.axis_index("narrow")
    column = lax.broadcasted_iota(jnp.int32, (1, width, channels), 1)
    left = (part > 0).astype(jnp.int32)
    right = (part < lax.axis_size("narrow") - 1).astype(jnp.int32)
    keep = (column < fine_cols + right) | (column >= width - left)

    def first_conv(index, carry):
        first = index * rows_one
        total = convolve(padded, first, rows_one, wide_one)
        for half in range(2):
            piece = total[:, :, half * channels : (half + 1) * channels]
            piece = silu(rms_scaled(piece, gain_two[...]))
            piece = jnp.where(keep, piece, 0.0).astype(jnp.bfloat16)
            for pair in range(rows_one // 2):
                second[first + 2 * pair + half] = piece[pair]
        return carry

    lax.fori_loop(0, (fine_rows + 2) // rows_one, first_conv, 0)

    @pl.when(band == 0)
    def _():
        second[0] = jnp.zeros((width, channels), jnp.bfloat16)

    @pl.when(band == lax.axis_size("wide") - 1)
    def _():
        second[fine_rows + 1] = jnp.zeros((width, channels), jnp.bfloat16)

    def second_conv(index, carry):
        first = index * rows_two
        total = convolve(second, first, rows_two, wide_two)
        for half in range(2):
            for pair in range(rows_two // 2):
                row = first + 2 * pair + half
                piece = total[pair, :fine_cols, half * channels : (half + 1) * channels]
                piece = piece + carried[row].astype(jnp.float32)
                out[row] = rms_scaled(piece, gain_out[...]).astype(jnp.bfloat16)
        return carry

    lax.fori_loop(0, fine_rows // rows_two, second_conv, 0)


def convolutions(active, above, below, side, carried, taps_one, taps_two, gain_two, gain_out):
    fine_rows, fine_cols, channels = active.shape
    width = fine_cols + SIDE
    vmem = pl.BlockSpec(memory_space=pltpu.VMEM)
    return pl.pallas_call(
        functools.partial(conv_kernel, rows_one=10, rows_two=16),
        out_shape=jax.ShapeDtypeStruct(active.shape, jnp.bfloat16),
        in_specs=[vmem] * 9,
        out_specs=vmem,
        scratch_shapes=[
            pltpu.VMEM((fine_rows + 4, width, channels), jnp.bfloat16),
            pltpu.VMEM((fine_rows + 2, width, channels), jnp.bfloat16),
            pltpu.VMEM((3, 4 * channels, 2 * channels), jnp.bfloat16),
            pltpu.VMEM((3, 4 * channels, 2 * channels), jnp.bfloat16),
        ],
        compiler_params=pltpu.CompilerParams(vmem_limit_bytes=56 * 1024 * 1024),
        name="convolutions",
    )(active, above, below, side, carried, taps_one, taps_two, gain_two, gain_out)


def from_both(cells, axis, dim, width):
    count = lax.axis_size(axis)
    ends = count - 1
    head = lax.slice_in_dim(cells, 0, width, axis=dim)
    tail = lax.slice_in_dim(cells, cells.shape[dim] - width, cells.shape[dim], axis=dim)
    before = lax.ppermute(tail, axis, [(i, i + 1) for i in range(ends)])
    after = lax.ppermute(head, axis, [(i + 1, i) for i in range(ends)])
    return before, after


def on_device(
    coarse,
    wanted,
    intersection,
    intersection_count,
    regrid_weight,
    reference_patch,
    patch_index,
    query_weight,
    key_value_weight,
    out_weight,
    conv_one,
    conv_two,
    gain_one,
    gain_two,
    gain_out,
):
    slot_count = wanted.shape[3]
    channels = coarse.shape[2]
    fine_rows, fine_cols, entries, block_cells = regrid_weight.shape
    every_block, group_patch = gather(coarse, reference_patch)
    carried, active = attend(
        wanted.reshape(-1),
        intersection.reshape(-1),
        intersection_count.reshape(-1),
        patch_index.reshape(-1),
        regrid_weight.reshape(fine_rows * fine_cols, entries, block_cells),
        every_block,
        group_patch,
        query_weight,
        key_value_weight,
        out_weight,
        gain_one.reshape(1, channels),
        coarse.shape[0],
        slot_count,
        fine_cols,
    )
    carried = carried.reshape(fine_rows, fine_cols, channels)
    active = active.reshape(fine_rows, fine_cols, channels)
    above, below = from_both(active, "wide", 0, 2)
    edges = jnp.concatenate(
        [
            jnp.concatenate([rows[:, :2], rows[:, fine_cols - 2 :]], axis=1)
            for rows in (above, active, below)
        ],
        axis=0,
    )
    before, after = from_both(edges, "narrow", 1, 2)
    middle = jnp.zeros((fine_rows + 4, SIDE - 4, channels), jnp.bfloat16)
    side = jnp.concatenate([after, middle, before], axis=1)
    return convolutions(
        active,
        above,
        below,
        side,
        carried,
        conv_one,
        conv_two,
        gain_two.reshape(1, channels),
        gain_out.reshape(1, channels),
    )


def solution(mesh):
    placed = (
        P(("members", "wide"), None, None),
        P("wide", "narrow", None, None),
        P("wide", "narrow", None),
        P("wide", "narrow"),
        P("wide", "narrow", None, None),
        P(("wide", "narrow"), None, None),
        P("wide", "narrow"),
        P(),
        P(),
        P(),
        P(),
        P(),
        P(),
        P(),
        P(),
    )
    return jax.shard_map(
        on_device,
        mesh=mesh,
        in_specs=placed,
        out_specs=P(("members", "wide"), "narrow", None),
        check_vma=False,
    )
```
